32 devices in a mesh: ulysses: 2 (over x), context: 16 (over z, y, core).
Axes of the slice: x: 2, y: 2, z: 4, core: 2. Of those that a mesh axis runs over, the one named last changes fastest.
Arguments:
- queries: bfloat16 [3072, 5120], P(('context', 'ulysses')), may hold values from -7 to 7
- key_vectors: bfloat16 [3072, 5120], P(('context', 'ulysses')), may hold values from -7 to 7
- value_vectors: bfloat16 [3072, 5120], P(('context', 'ulysses')), may hold values from -6 to 6
- labels: int32 [40], replicated, may hold values from 0 to 1, as said below
- block_lists: int32 [40, 48, 5], replicated, may hold values from 0 to 47, as said below
- counts: int32 [40, 48], replicated, may hold values from 1 to 5, as said below
- query_scale: float32 [40], replicated, may hold values from 1.5 to 3
- key_scale: float32 [40], replicated, may hold values from 1.5 to 3
- value_scale: float32 [40], replicated, may hold values from 0.5 to 2
Outputs:
- attended: bfloat16 [3072, 5120], P(('context', 'ulysses'))
The draws below stay inside these ranges and needn't reach their ends.
Inputs may be any that keep to these rules, and one draw needn't show every extreme that they name: `labels`: exactly 16 entries are 1, the others 0; every aligned run of 20 heads holds at least one 0. Every entry of block_lists[h, b] lies within 2 blocks of b; the first entry is b itself and the first counts[h, b] entries are distinct. counts[h, b] is at least one less than and at most the number of blocks of the clip within 2 blocks of b; every head has a query block that uses all 5 entries.
All inputs are finite; a program needn't handle non-finite values.
Results may differ from the reference program's by a relative error of at most 0.0024.
Values may be sent and summed in bfloat16 or wider, within the bound.
A program may use at most 128 MiB of HBM per device.

```python
import math
import jax
import jax.numpy as jnp
from jax import lax

HEADS = 40
HEAD_DIM = 128
FRAMES = 16
TEMPORAL = 16
MARGIN = 2
BLOCK = 64
HEADS_DEV = 20
POSITIONS = 192
SEQ = 3072
SHARD_BLOCKS = 3
QUERY_BLOCKS = 48
KEY_BLOCKS = 5


def make_labels(key):
    first_key, second_key = jax.random.split(key)
    group_raw = jax.random.randint(first_key, (HEADS // HEADS_DEV, HEADS_DEV), 0, 2 ** 20)
    group_scores = group_raw * HEADS_DEV + jnp.arange(HEADS_DEV, dtype=jnp.int32)[None, :]
    group_ranks = jnp.argsort(jnp.argsort(group_scores, axis=1), axis=1)
    forced = (group_ranks == 0).reshape(HEADS)
    head_iota = jnp.arange(HEADS, dtype=jnp.int32)
    raw = jax.random.randint(second_key, (HEADS,), 0, 2 ** 20)
    scores = raw * HEADS + head_iota
    scores = jnp.where(forced, -1 - head_iota, scores)
    ranking = jnp.argsort(jnp.argsort(-scores))
    return (ranking < TEMPORAL).astype(jnp.int32)


def draw_labels(key, part):
    return make_labels(jax.random.fold_in(key, 11))


def list_parts(key):
    offsets = jnp.arange(KEY_BLOCKS, dtype=jnp.int32) - MARGIN
    query_ids = jnp.arange(QUERY_BLOCKS, dtype=jnp.int32)
    candidate = query_ids[:, None] + offsets[None, :]
    inside = (candidate >= 0) & (candidate < QUERY_BLOCKS)
    allowed = jnp.broadcast_to(inside[None], (HEADS, QUERY_BLOCKS, KEY_BLOCKS))
    return (query_ids, offsets, candidate, allowed)


def draw_block_lists(key, part):
    query_ids, offsets, candidate, allowed = list_parts(key)
    index_row = jnp.arange(KEY_BLOCKS, dtype=jnp.int32)
    raw = jax.random.randint(jax.random.fold_in(key, 12), (HEADS, QUERY_BLOCKS, KEY_BLOCKS), 0, 2 ** 20)
    scores = raw * KEY_BLOCKS + index_row
    scores = jnp.where((offsets == 0)[None, None, :], 2 ** 30, scores)
    scores = jnp.where(allowed, scores, -1 - index_row)
    _, picked = lax.top_k(scores, KEY_BLOCKS)
    full_candidate = jnp.broadcast_to(candidate[None], (HEADS, QUERY_BLOCKS, KEY_BLOCKS))
    picked_candidate = jnp.take_along_axis(full_candidate, picked, axis=2)
    picked_allowed = jnp.take_along_axis(allowed, picked, axis=2)
    return jnp.where(picked_allowed, picked_candidate, query_ids[None, :, None]).astype(jnp.int32)


def draw_counts(key, part):
    query_ids, offsets, candidate, allowed = list_parts(key)
    room = jnp.sum(allowed.astype(jnp.int32), axis=-1)
    first_key, second_key = jax.random.split(jax.random.fold_in(key, 13))
    lowest = jnp.maximum(room - 1, 1)
    drawn = jax.random.randint(first_key, (HEADS, QUERY_BLOCKS), lowest, room + 1)
    chosen = jax.random.randint(second_key, (HEADS, 1), MARGIN, QUERY_BLOCKS - MARGIN)
    full_row = query_ids[None, :] == chosen
    return jnp.where(full_row, room, drawn).astype(jnp.int32)


def draw_queries(key, part):
    base_key = jax.random.fold_in(key, 21)
    drawn = jnp.clip(jax.random.normal(base_key, (SEQ, HEADS, HEAD_DIM)), -6.0, 6.0)
    return drawn.reshape(SEQ, HEADS * HEAD_DIM).astype(jnp.bfloat16)


def draw_key_vectors(key, part):
    base_key = jax.random.fold_in(key, 22)
    drawn = jnp.clip(jax.random.normal(base_key, (SEQ, HEADS, HEAD_DIM)), -6.0, 6.0)
    return drawn.reshape(SEQ, HEADS * HEAD_DIM).astype(jnp.bfloat16)


def steps_of(stream_key, dims, pieces, low, high):
    factor_of = 1.0
    for axis_at, parts in pieces:
        draws = jax.random.uniform(jax.random.fold_in(jax.random.fold_in(stream_key, 6), axis_at), (parts,), jnp.float32, low / len(pieces), high / len(pieces))
        factor_of = factor_of * jnp.repeat(jnp.exp(draws), dims[axis_at] // parts).reshape((-1,) + (1,) * (len(dims) - 1 - axis_at))
    return factor_of


def noise(rng, shape, width, most, cuts=(), held_as=jnp.bfloat16):
    values = width * jax.random.normal(rng, shape, jnp.float32)
    if cuts:
        values = values * steps_of(rng, shape, cuts, -0.22, 0.18)
    return jnp.clip(values, -most, most).astype(held_as)


def setup_inputs(seed: int = 0) -> dict:
    key_of = jax.random.split(jax.random.key(seed), 10)
    queries = draw_queries(jax.random.fold_in(key_of[9], 71), 0)
    key_vectors = draw_key_vectors(jax.random.fold_in(key_of[9], 71), 0)
    value_vectors = noise(key_of[2], (SEQ, HEADS * HEAD_DIM), 1.0, 6.0, ((0, 32),))
    labels = draw_labels(jax.random.fold_in(key_of[9], 71), 0)
    block_lists = draw_block_lists(jax.random.fold_in(key_of[9], 71), 0)
    counts = draw_counts(jax.random.fold_in(key_of[9], 71), 0)
    query_scale = jnp.clip(jnp.exp(jax.random.uniform(key_of[6], (HEADS,), jnp.float32, math.log(1.5), math.log(3.0))), 1.5, 3.0)
    key_scale = jnp.clip(jnp.exp(jax.random.uniform(key_of[7], (HEADS,), jnp.float32, math.log(1.5), math.log(3.0))), 1.5, 3.0)
    value_scale = jnp.clip(jnp.exp(jax.random.uniform(key_of[8], (HEADS,), jnp.float32, math.log(0.5), math.log(2.0))), 0.5, 2.0)
    return {"queries": queries, "key_vectors": key_vectors, "value_vectors": value_vectors, "labels": labels, "block_lists": block_lists, "counts": counts, "query_scale": query_scale, "key_scale": key_scale, "value_scale": value_scale}


def reorder(column, temporal):
    position_major = column.reshape(FRAMES, POSITIONS, HEAD_DIM).transpose(1, 0, 2).reshape(SEQ, HEAD_DIM)
    return jnp.where(temporal == 1, position_major, column)

def restore(column, temporal):
    frame_major = column.reshape(POSITIONS, FRAMES, HEAD_DIM).transpose(1, 0, 2).reshape(SEQ, HEAD_DIM)
    return jnp.where(temporal == 1, frame_major, column)

def group_attend(query_tiles, key_blocks, value_blocks, chosen, allowed, logit_scale, value_factor):
    group = query_tiles.shape[0]
    collected_keys = key_blocks[chosen].reshape(group, KEY_BLOCKS * BLOCK, HEAD_DIM)
    collected_values = value_blocks[chosen].reshape(group, KEY_BLOCKS * BLOCK, HEAD_DIM)
    attention_logits = jnp.einsum('fac,foc->fao', query_tiles.astype(jnp.float32), collected_keys.astype(jnp.float32), precision=lax.Precision.HIGHEST) * logit_scale
    valid = jnp.repeat(jnp.arange(KEY_BLOCKS)[None, :] < allowed[:, None], BLOCK, axis=1)
    attention_logits = jnp.where(valid[:, None, :], attention_logits, -jnp.inf)
    peak = lax.optimization_barrier(jnp.max(attention_logits, axis=-1, keepdims=True))
    weight = jnp.exp(attention_logits - peak)
    total = lax.optimization_barrier(jnp.sum(weight, axis=-1, keepdims=True))
    weight_second = lax.optimization_barrier(weight.astype(jnp.bfloat16))
    blended_output = jnp.einsum('oem,omg->oeg', weight_second.astype(jnp.float32), collected_values.astype(jnp.float32), precision=lax.Precision.HIGHEST)
    return (blended_output * (value_factor / total)).astype(jnp.bfloat16)

def reference(queries, key_vectors, value_vectors, labels, block_lists, counts, query_scale, key_scale, value_scale):
    group_count = QUERY_BLOCKS // SHARD_BLOCKS

    def one_head(head_index):
        temporal = labels[head_index]
        start = head_index * HEAD_DIM
        query_column = reorder(lax.dynamic_slice_in_dim(queries, start, HEAD_DIM, 1), temporal)
        key_column = reorder(lax.dynamic_slice_in_dim(key_vectors, start, HEAD_DIM, 1), temporal)
        value_column = reorder(lax.dynamic_slice_in_dim(value_vectors, start, HEAD_DIM, 1), temporal)
        query_groups = query_column.reshape(group_count, SHARD_BLOCKS, BLOCK, HEAD_DIM)
        key_blocks = key_column.reshape(QUERY_BLOCKS, BLOCK, HEAD_DIM)
        value_blocks = value_column.reshape(QUERY_BLOCKS, BLOCK, HEAD_DIM)
        list_groups = block_lists[head_index].reshape(group_count, SHARD_BLOCKS, KEY_BLOCKS)
        count_groups = counts[head_index].reshape(group_count, SHARD_BLOCKS)
        logit_scale = query_scale[head_index] * key_scale[head_index] / math.sqrt(HEAD_DIM)
        value_factor = value_scale[head_index]

        def per_group(items):
            return group_attend(items[0], key_blocks, value_blocks, items[1], items[2], logit_scale, value_factor)
        outputs = lax.map(per_group, (query_groups, list_groups, count_groups))
        return restore(outputs.reshape(SEQ, HEAD_DIM), temporal)
    result = lax.map(one_head, jnp.arange(HEADS, dtype=jnp.int32))
    return result.transpose(1, 0, 2).reshape(SEQ, HEADS * HEAD_DIM)
```

```python
import functools
import math

import jax
import jax.numpy as jnp
from jax import lax
from jax.experimental import pallas as pl
from jax.experimental.pallas import tpu as pltpu
from jax.sharding import PartitionSpec as P

FRAMES = 16
TEMPORAL = 16
MARGIN = 2
BLOCK = 64
WIDTH = 128
GROUP = 8
RIM = MARGIN * BLOCK
PAIR = 2 * BLOCK
WINDOW = PAIR + 2 * RIM
MASKED = -1e30


def pack(
    labels,
    query_scale,
    key_scale,
    value_scale,
    bits,
    q_ref,
    k_ref,
    v_ref,
    packed,
    place,
    sorted_bits,
    logit_scale,
    value_factor,
):
    heads = labels.shape[0]

    def one(head, spatial):
        temporal = labels[head]
        slot = jnp.where(temporal == 1, heads - TEMPORAL + head - spatial, spatial)
        place[head] = slot
        logit_scale[slot] = query_scale[head] * key_scale[head] * (1.0 / math.sqrt(WIDTH))
        value_factor[slot] = value_scale[head]
        sorted_bits[pl.ds(slot, 1), :] = bits[pl.ds(head, 1), :]
        columns = pl.ds(pl.multiple_of(head * WIDTH, WIDTH), WIDTH)
        packed[slot, :, 0:WIDTH] = q_ref[:, columns]
        packed[slot, :, WIDTH : 2 * WIDTH] = k_ref[:, columns]
        packed[slot, :, 2 * WIDTH : 3 * WIDTH] = v_ref[:, columns]
        return spatial + 1 - temporal

    lax.fori_loop(0, heads, one, 0)


def unpack(place, returned, out_ref):
    def one(head, carry):
        columns = pl.ds(pl.multiple_of(head * WIDTH, WIDTH), WIDTH)
        out_ref[:, columns] = returned[place[head]]
        return carry

    lax.fori_loop(0, place.shape[0], one, 0)


def kernel(
    devices,
    ulysses,
    bits,
    logit_scale,
    value_scale,
    packed,
    returned,
    near,
    frames,
    lines,
    near_out,
    line_out,
    frame_out,
    swap,
    near_send,
    near_recv,
    far_send,
    far_recv,
    rim_send,
    rim_recv,
    own_sem,
    near_back_send,
    near_back_recv,
    far_back_send,
    far_back_recv,
):
    heads, rows = packed.shape[:2]
    spatial = heads - TEMPORAL
    share = spatial // GROUP
    near_rows = GROUP * rows
    line_rows = FRAMES * rows
    per_frame = devices // FRAMES
    groups = devices // GROUP
    near_pairs = near_rows // PAIR
    line_pairs = line_rows // PAIR
    tile = 16
    strip = tile * FRAMES
    strips = rows // tile

    me = lax.axis_index("context") * ulysses + lax.axis_index("ulysses")
    slot = lax.rem(me, GROUP)
    base = me - slot
    group = lax.div(me, GROUP)
    frame = lax.div(me, per_frame)
    chunk = lax.rem(me, per_frame)

    def device(index):
        return (lax.rem(index, ulysses), lax.div(index, ulysses))

    def near_peer(step):
        return lax.rem(slot + step, GROUP)

    def far_peer(step):
        return lax.rem(frame + step, FRAMES)

    has_lower = group > 0
    has_upper = group < groups - 1
    line_lower = chunk > 0
    line_upper = chunk < per_frame - 1
    mesh_id = pl.DeviceIdType.MESH

    barrier = pltpu.get_barrier_semaphore()

    def greet(index):
        pl.semaphore_signal(barrier, inc=1, device_id=device(index), device_id_type=mesh_id)

    for step in range(1, GROUP):
        greet(base + near_peer(step))
    for step in range(1, FRAMES):
        greet(far_peer(step) * per_frame + chunk)
    for away in (GROUP, 1):
        greet(lax.rem(me + away, devices))
        greet(lax.rem(me + devices - away, devices))
    pl.semaphore_wait(barrier, GROUP - 1 + FRAMES - 1 + 4)

    def near_copy(peer, source):
        return pltpu.make_async_remote_copy(
            src_ref=packed.at[pl.ds(share * peer, share)],
            dst_ref=near.at[:, pl.ds(RIM + rows * source, rows), :],
            send_sem=near_send.at[peer],
            recv_sem=near_recv.at[source],
            device_id=device(base + peer),
            device_id_type=mesh_id,
        )

    def far_copy(peer, source):
        return pltpu.make_async_remote_copy(
            src_ref=packed.at[spatial + peer],
            dst_ref=frames.at[source],
            send_sem=far_send.at[peer],
            recv_sem=far_recv.at[source],
            device_id=device(peer * per_frame + chunk),
            device_id_type=mesh_id,
        )

    for step in range(1, FRAMES):
        far_copy(far_peer(step), frame).start()
        if step < GROUP:
            near_copy(near_peer(step), slot).start()
    own_near = pltpu.make_async_copy(
        packed.at[pl.ds(share * slot, share)],
        near.at[:, pl.ds(RIM + rows * slot, rows), :],
        own_sem.at[0],
    )
    own_far = pltpu.make_async_copy(packed.at[spatial + frame], frames.at[frame], own_sem.at[1])
    own_near.start()
    own_far.start()

    turned = lax.broadcasted_iota(jnp.int32, (strip, strip), 0)
    across = lax.broadcasted_iota(jnp.int32, (strip, strip), 1)
    swap[...] = jnp.where(
        across == lax.rem(turned, tile) * tile + lax.div(turned, tile), 1.0, 0.0
    ).astype(jnp.bfloat16)

    rim_lanes = pl.ds(WIDTH, 2 * WIDTH)

    @pl.when(jnp.logical_not(has_lower))
    def _():
        near[:, 0:RIM, :] = jnp.zeros((share, RIM, 3 * WIDTH), jnp.bfloat16)

    @pl.when(jnp.logical_not(has_upper))
    def _():
        near[:, RIM + near_rows :, :] = jnp.zeros((share, RIM, 3 * WIDTH), jnp.bfloat16)

    @pl.when(jnp.logical_not(line_lower))
    def _():
        lines[0:RIM, :] = jnp.zeros((RIM, 3 * WIDTH), jnp.bfloat16)

    @pl.when(jnp.logical_not(line_upper))
    def _():
        lines[RIM + line_rows :, :] = jnp.zeros((RIM, 3 * WIDTH), jnp.bfloat16)

    def rim_copy(which, peer):
        source = (near_rows, RIM, line_rows, RIM)[which]
        target = (0, RIM + near_rows, 0, RIM + line_rows)[which]
        if which < 2:
            src = near.at[:, pl.ds(source, RIM), rim_lanes]
            dst = near.at[:, pl.ds(target, RIM), rim_lanes]
        else:
            src = lines.at[pl.ds(source, RIM), rim_lanes]
            dst = lines.at[pl.ds(target, RIM), rim_lanes]
        return pltpu.make_async_remote_copy(
            src_ref=src,
            dst_ref=dst,
            send_sem=rim_send.at[which],
            recv_sem=rim_recv.at[which],
            device_id=device(peer),
            device_id_type=mesh_id,
        )

    rims = (
        (has_upper, me + GROUP, has_lower),
        (has_lower, me - GROUP, has_upper),
        (line_upper, me + 1, line_lower),
        (line_lower, me - 1, line_upper),
    )

    def send_rim(which):
        @pl.when(rims[which][0])
        def _():
            rim_copy(which, rims[which][1]).start()

    def await_rim(which):
        @pl.when(rims[which][2])
        def _():
            rim_copy(which, me).wait_recv()

    key_block = lax.div(lax.broadcasted_iota(jnp.int32, (1, WINDOW), 1), BLOCK)
    key_bit = jnp.left_shift(jnp.ones_like(key_block), key_block)

    def attend(queries, keys, values, head, block):
        lower = jnp.where((key_bit & bits[head, block]) != 0, 0.0, MASKED)
        upper = jnp.where((key_bit & (bits[head, block + 1] * 2)) != 0, 0.0, MASKED)
        bias = jnp.concatenate(
            [
                jnp.broadcast_to(lower, (BLOCK, WINDOW)),
                jnp.broadcast_to(upper, (BLOCK, WINDOW)),
            ],
            axis=0,
        )
        score = lax.dot_general(
            queries, keys, (((1,), (1,)), ((), ())), preferred_element_type=jnp.float32
        )
        score = score * logit_scale[head] + bias
        peak = jnp.max(score, axis=-1, keepdims=True)
        weight = jnp.exp(score - peak)
        total = jnp.sum(weight, axis=-1, keepdims=True)
        mixed = jnp.dot(
            weight.astype(jnp.bfloat16), values, preferred_element_type=jnp.float32
        )
        return (mixed * (value_scale[head] / total)).astype(jnp.bfloat16)

    def near_pair(i, pair):
        start = pl.multiple_of(pair * PAIR, PAIR)
        head = share * slot + i
        near_out[i, pl.ds(start, PAIR), :] = attend(
            near[i, pl.ds(start + RIM, PAIR), 0:WIDTH],
            near[i, pl.ds(start, WINDOW), WIDTH : 2 * WIDTH],
            near[i, pl.ds(start, WINDOW), 2 * WIDTH : 3 * WIDTH],
            head,
            group * (near_rows // BLOCK) + 2 * pair,
        )

    line_head = spatial + frame

    def line_pair(pair):
        start = pl.multiple_of(pair * PAIR, PAIR)
        line_out[pl.ds(start, PAIR), :] = attend(
            lines[pl.ds(start + RIM, PAIR), 0:WIDTH],
            lines[pl.ds(start, WINDOW), WIDTH : 2 * WIDTH],
            lines[pl.ds(start, WINDOW), 2 * WIDTH : 3 * WIDTH],
            line_head,
            chunk * (line_rows // BLOCK) + 2 * pair,
        )

    for step in range(1, GROUP):
        near_copy(near_peer(step), near_peer(step)).wait_recv()
    own_near.wait()
    send_rim(0)
    send_rim(1)

    def near_middle(n, carry):
        for i in range(share):
            near_pair(i, n + 1)
        return carry

    lax.fori_loop(0, near_pairs - 2, near_middle, 0)

    for step in range(1, FRAMES):
        far_copy(far_peer(step), far_peer(step)).wait_recv()
    own_far.wait()

    def turn(s, carry):
        piece = frames[:, pl.ds(pl.multiple_of(s * tile, tile), tile), :]
        lines[pl.ds(pl.multiple_of(RIM + s * strip, RIM), strip), :] = jnp.dot(
            swap[...], piece.reshape(strip, 3 * WIDTH), preferred_element_type=jnp.float32
        ).astype(jnp.bfloat16)
        return carry

    lax.fori_loop(0, strips, turn, 0)
    send_rim(2)
    send_rim(3)

    await_rim(0)
    await_rim(1)

    def near_edge(i, carry):
        near_pair(i, 0)
        near_pair(i, near_pairs - 1)
        return carry

    lax.fori_loop(0, share, near_edge, 0)

    def near_back(peer, source):
        return pltpu.make_async_remote_copy(
            src_ref=near_out.at[:, pl.ds(rows * peer, rows), :],
            dst_ref=returned.at[pl.ds(share * source, share)],
            send_sem=near_back_send.at[peer],
            recv_sem=near_back_recv.at[source],
            device_id=device(base + peer),
            device_id_type=mesh_id,
        )

    def far_back(peer, source):
        return pltpu.make_async_remote_copy(
            src_ref=frame_out.at[peer],
            dst_ref=returned.at[spatial + source],
            send_sem=far_back_send.at[peer],
            recv_sem=far_back_recv.at[source],
            device_id=device(peer * per_frame + chunk),
            device_id_type=mesh_id,
        )

    for step in range(1, GROUP):
        near_back(near_peer(step), slot).start()
    own_near_back = pltpu.make_async_copy(
        near_out.at[:, pl.ds(rows * slot, rows), :],
        returned.at[pl.ds(share * slot, share)],
        own_sem.at[2],
    )
    own_near_back.start()

    def line_middle(n, carry):
        line_pair(2 * n + 1)
        line_pair(2 * n + 2)
        return carry

    lax.fori_loop(0, (line_pairs - 2) // 2, line_middle, 0)
    await_rim(2)
    await_rim(3)
    line_pair(0)
    line_pair(line_pairs - 1)

    def turn_back(s, carry):
        piece = jnp.dot(
            swap[...],
            line_out[pl.ds(pl.multiple_of(s * strip, strip), strip), :],
            preferred_element_type=jnp.float32,
        ).astype(jnp.bfloat16)
        frame_out[:, pl.ds(pl.multiple_of(s * tile, tile), tile), :] = piece.reshape(
            FRAMES, tile, WIDTH
        )
        return carry

    lax.fori_loop(0, strips, turn_back, 0)
    for step in range(1, FRAMES):
        far_back(far_peer(step), frame).start()
    own_far_back = pltpu.make_async_copy(
        frame_out.at[frame], returned.at[spatial + frame], own_sem.at[3]
    )
    own_far_back.start()

    for step in range(1, GROUP):
        near_copy(near_peer(step), slot).wait_send()
        near_back(near_peer(step), slot).wait_send()
        near_back(near_peer(step), near_peer(step)).wait_recv()
    for which in range(4):

        @pl.when(rims[which][0])
        def _(which=which):
            rim_copy(which, rims[which][1]).wait_send()

    own_near_back.wait()
    for step in range(1, FRAMES):
        far_copy(far_peer(step), frame).wait_send()
        far_back(far_peer(step), frame).wait_send()
        far_back(far_peer(step), far_peer(step)).wait_recv()
    own_far_back.wait()


def shards(
    devices,
    queries,
    key_vectors,
    value_vectors,
    labels,
    block_lists,
    counts,
    query_scale,
    key_scale,
    value_scale,
):
    rows, width = queries.shape
    heads = labels.shape[0]
    blocks = counts.shape[1]
    spatial = heads - TEMPORAL
    share = spatial // GROUP
    ulysses = lax.axis_size("ulysses")

    entries = jnp.arange(block_lists.shape[2], dtype=jnp.int32)
    offsets = block_lists - jnp.arange(blocks, dtype=jnp.int32)[None, :, None] + MARGIN
    bits = jnp.sum(
        jnp.where(entries < counts[:, :, None], jnp.left_shift(1, offsets), 0), axis=2
    ).astype(jnp.int32)

    near_rows = GROUP * rows
    line_rows = FRAMES * rows
    bf16 = jnp.bfloat16
    smem = pl.BlockSpec(memory_space=pltpu.SMEM)
    vmem = pl.BlockSpec(memory_space=pltpu.VMEM)
    anywhere = pl.BlockSpec(memory_space=pl.ANY)
    packed, place, sorted_bits, logit_scale, value_factor = pl.pallas_call(
        pack,
        out_shape=(
            jax.ShapeDtypeStruct((heads, rows, 3 * WIDTH), bf16),
            jax.ShapeDtypeStruct((heads,), jnp.int32),
            jax.ShapeDtypeStruct((heads, blocks), jnp.int32),
            jax.ShapeDtypeStruct((heads,), jnp.float32),
            jax.ShapeDtypeStruct((heads,), jnp.float32),
        ),
        in_specs=[smem] * 4 + [vmem] * 4,
        out_specs=(vmem, smem, vmem, smem, smem),
        compiler_params=pltpu.CompilerParams(vmem_limit_bytes=40 * 1024 * 1024),
    )(
        labels,
        query_scale,
        key_scale,
        value_scale,
        bits,
        queries,
        key_vectors,
        value_vectors,
    )
    returned = pl.pallas_call(
        functools.partial(kernel, devices, ulysses),
        out_shape=jax.ShapeDtypeStruct((heads, rows, WIDTH), bf16),
        in_specs=[smem] * 3 + [anywhere],
        out_specs=anywhere,
        scratch_shapes=[
            pltpu.VMEM((share, near_rows + 2 * RIM, 3 * WIDTH), bf16),
            pltpu.VMEM((FRAMES, rows, 3 * WIDTH), bf16),
            pltpu.VMEM((line_rows + 2 * RIM, 3 * WIDTH), bf16),
            pltpu.VMEM((share, near_rows, WIDTH), bf16),
            pltpu.VMEM((line_rows, WIDTH), bf16),
            pltpu.VMEM((FRAMES, rows, WIDTH), bf16),
            pltpu.VMEM((16 * FRAMES, 16 * FRAMES), bf16),
            pltpu.SemaphoreType.DMA((GROUP,)),
            pltpu.SemaphoreType.DMA((GROUP,)),
            pltpu.SemaphoreType.DMA((FRAMES,)),
            pltpu.SemaphoreType.DMA((FRAMES,)),
            pltpu.SemaphoreType.DMA((4,)),
            pltpu.SemaphoreType.DMA((4,)),
            pltpu.SemaphoreType.DMA((4,)),
            pltpu.SemaphoreType.DMA((GROUP,)),
            pltpu.SemaphoreType.DMA((GROUP,)),
            pltpu.SemaphoreType.DMA((FRAMES,)),
            pltpu.SemaphoreType.DMA((FRAMES,)),
        ],
        compiler_params=pltpu.CompilerParams(
            collective_id=0, has_side_effects=True, vmem_limit_bytes=40 * 1024 * 1024
        ),
        cost_estimate=pl.CostEstimate(
            flops=10**9, bytes_accessed=4 * rows * width * 2, transcendentals=10**6
        ),
    )(sorted_bits, logit_scale, value_factor, packed)
    return pl.pallas_call(
        unpack,
        out_shape=jax.ShapeDtypeStruct((rows, width), bf16),
        in_specs=[smem, vmem],
        out_specs=vmem,
    )(place, returned)


def solution(mesh):
    tokens = P(("context", "ulysses"), None)
    devices = mesh.shape["ulysses"] * mesh.shape["context"]
    return jax.shard_map(
        functools.partial(shards, devices),
        mesh=mesh,
        in_specs=(tokens, tokens, tokens, P(), P(), P(), P(), P(), P()),
        out_specs=tokens,
        check_vma=False,
    )
```

```python
import functools
import math

import jax
import jax.numpy as jnp
from jax import lax
from jax.experimental import pallas as pl
from jax.experimental.pallas import tpu as pltpu
from jax.sharding import PartitionSpec as P

FRAMES = 16
TEMPORAL = 16
MARGIN = 2
BLOCK = 64
WIDTH = 128
GROUP = 8
RIM = MARGIN * BLOCK
PAIR = 2 * BLOCK
WINDOW = PAIR + 2 * RIM
MASKED = -1e30


def slot_of(labels, head, spatial):
    temporal = labels[head]
    slot = jnp.where(temporal == 1, labels.shape[0] - TEMPORAL + head - spatial, spatial)
    return slot, spatial + 1 - temporal


def pack(
    labels_in,
    query_scale_in,
    key_scale_in,
    value_scale_in,
    lists_in,
    counts_in,
    q_in,
    k_in,
    v_in,
    packed,
    table,
    labels,
    query_scale,
    key_scale,
    value_scale,
    lists,
    counts,
    bits,
    sems,
    packed_sem,
):
    heads = labels_in.shape[0]
    small = [
        pltpu.make_async_copy(source, target, sems.at[i])
        for i, (source, target) in enumerate(
            (
                (labels_in, labels),
                (query_scale_in, query_scale),
                (key_scale_in, key_scale),
                (value_scale_in, value_scale),
                (lists_in, lists),
                (counts_in, counts),
            )
        )
    ]
    for copy in small:
        copy.start()
    small[0].wait()

    def move(head, spatial):
        slot, after = slot_of(labels, head, spatial)
        columns = pl.ds(pl.multiple_of(head * WIDTH, WIDTH), WIDTH)
        for i, source in enumerate((q_in, k_in, v_in)):
            pltpu.make_async_copy(
                source.at[:, columns],
                packed.at[slot, :, pl.ds(i * WIDTH, WIDTH)],
                packed_sem,
            ).start()
        return after

    lax.fori_loop(0, heads, move, 0, unroll=4)
    for copy in small[1:]:
        copy.wait()

    query_ids = lax.broadcasted_iota(jnp.int32, counts.shape, 1)
    total = jnp.zeros(counts.shape, jnp.int32)
    for j in range(lists.shape[0]):
        offset = lists[j] - query_ids + MARGIN
        total += jnp.where(counts[...] > j, jnp.left_shift(jnp.ones_like(offset), offset), 0)
    bits[:, 0 : counts.shape[1]] = total.astype(jnp.float32)
    lane = lax.broadcasted_iota(jnp.int32, (1, table.shape[1]), 1)

    def sort(head, spatial):
        slot, after = slot_of(labels, head, spatial)
        scale = query_scale[head] * key_scale[head] * (1.0 / math.sqrt(WIDTH))
        row = pl.ds(slot, 1)
        table[row, :] = jnp.where(
            lane < counts.shape[1],
            bits[pl.ds(head, 1), :],
            jnp.where(lane == table.shape[1] - WIDTH, scale, value_scale[head]),
        )
        return after

    lax.fori_loop(0, heads, sort, 0)
    pltpu.make_async_copy(packed, packed, packed_sem).wait()


def unpack(labels_in, returned, out, labels, sem, out_sem):
    copy = pltpu.make_async_copy(labels_in, labels, sem)
    copy.start()
    copy.wait()

    def move(head, spatial):
        slot, after = slot_of(labels, head, spatial)
        columns = pl.ds(pl.multiple_of(head * WIDTH, WIDTH), WIDTH)
        pltpu.make_async_copy(returned.at[slot], out.at[:, columns], out_sem).start()
        return after

    lax.fori_loop(0, labels_in.shape[0], move, 0, unroll=4)
    pltpu.make_async_copy(out, out, out_sem).wait()


def kernel(
    devices,
    ulysses,
    table_in,
    packed,
    returned,
    table,
    near,
    frames,
    lines,
    near_out,
    line_out,
    frame_out,
    swap,
    near_send,
    near_recv,
    far_send,
    far_recv,
    rim_send,
    rim_recv,
    own_sem,
    near_back_send,
    near_back_recv,
    far_back_send,
    far_back_recv,
    small_sem,
):
    heads, rows = packed.shape[:2]
    spatial = heads - TEMPORAL
    share = spatial // GROUP
    near_rows = GROUP * rows
    line_rows = FRAMES * rows
    per_frame = devices // FRAMES
    groups = devices // GROUP
    near_pairs = near_rows // PAIR
    line_pairs = line_rows // PAIR
    tile = 16
    strip = tile * FRAMES
    strips = rows // tile

    me = lax.axis_index("context") * ulysses + lax.axis_index("ulysses")
    slot = lax.rem(me, GROUP)
    base = me - slot
    group = lax.div(me, GROUP)
    frame = lax.div(me, per_frame)
    chunk = lax.rem(me, per_frame)

    def device(index):
        return (lax.rem(index, ulysses), lax.div(index, ulysses))

    def near_peer(step):
        return lax.rem(slot + step, GROUP)

    def far_peer(step):
        return lax.rem(frame + step, FRAMES)

    has_lower = group > 0
    has_upper = group < groups - 1
    line_lower = chunk > 0
    line_upper = chunk < per_frame - 1
    mesh_id = pl.DeviceIdType.MESH

    table_copy = pltpu.make_async_copy(table_in, table, small_sem)
    table_copy.start()
    logit_at = table.shape[1] - WIDTH

    barrier = pltpu.get_barrier_semaphore()

    def greet(index):
        pl.semaphore_signal(barrier, inc=1, device_id=device(index), device_id_type=mesh_id)

    for step in range(1, GROUP):
        greet(base + near_peer(step))
    for step in range(1, FRAMES):
        greet(far_peer(step) * per_frame + chunk)
    for away in (GROUP, 1):
        greet(lax.rem(me + away, devices))
        greet(lax.rem(me + devices - away, devices))
    pl.semaphore_wait(barrier, GROUP - 1 + FRAMES - 1 + 4)

    def near_copy(peer, source):
        return pltpu.make_async_remote_copy(
            src_ref=packed.at[pl.ds(share * peer, share)],
            dst_ref=near.at[:, pl.ds(RIM + rows * source, rows), :],
            send_sem=near_send.at[peer],
            recv_sem=near_recv.at[source],
            device_id=device(base + peer),
            device_id_type=mesh_id,
        )

    def far_copy(peer, source):
        return pltpu.make_async_remote_copy(
            src_ref=packed.at[spatial + peer],
            dst_ref=frames.at[source],
            send_sem=far_send.at[peer],
            recv_sem=far_recv.at[source],
            device_id=device(peer * per_frame + chunk),
            device_id_type=mesh_id,
        )

    for step in range(1, GROUP):
        near_copy(near_peer(step), slot).start()
    for step in range(1, FRAMES):
        far_copy(far_peer(step), frame).start()
    own_near = pltpu.make_async_copy(
        packed.at[pl.ds(share * slot, share)],
        near.at[:, pl.ds(RIM + rows * slot, rows), :],
        own_sem.at[0],
    )
    own_far = pltpu.make_async_copy(packed.at[spatial + frame], frames.at[frame], own_sem.at[1])
    own_near.start()
    own_far.start()

    turned = lax.broadcasted_iota(jnp.int32, (strip, strip), 0)
    across = lax.broadcasted_iota(jnp.int32, (strip, strip), 1)
    swap[...] = jnp.where(
        across == lax.rem(turned, tile) * tile + lax.div(turned, tile), 1.0, 0.0
    ).astype(jnp.bfloat16)

    rim_lanes = pl.ds(WIDTH, 2 * WIDTH)

    @pl.when(jnp.logical_not(has_lower))
    def _():
        near[:, 0:RIM, :] = jnp.zeros((share, RIM, 3 * WIDTH), jnp.bfloat16)

    @pl.when(jnp.logical_not(has_upper))
    def _():
        near[:, RIM + near_rows :, :] = jnp.zeros((share, RIM, 3 * WIDTH), jnp.bfloat16)

    @pl.when(jnp.logical_not(line_lower))
    def _():
        lines[0:RIM, :] = jnp.zeros((RIM, 3 * WIDTH), jnp.bfloat16)

    @pl.when(jnp.logical_not(line_upper))
    def _():
        lines[RIM + line_rows :, :] = jnp.zeros((RIM, 3 * WIDTH), jnp.bfloat16)

    def rim_copy(which, peer):
        source = (near_rows, RIM, line_rows, RIM)[which]
        target = (0, RIM + near_rows, 0, RIM + line_rows)[which]
        if which < 2:
            src = near.at[:, pl.ds(source, RIM), rim_lanes]
            dst = near.at[:, pl.ds(target, RIM), rim_lanes]
        else:
            src = lines.at[pl.ds(source, RIM), rim_lanes]
            dst = lines.at[pl.ds(target, RIM), rim_lanes]
        return pltpu.make_async_remote_copy(
            src_ref=src,
            dst_ref=dst,
            send_sem=rim_send.at[which],
            recv_sem=rim_recv.at[which],
            device_id=device(peer),
            device_id_type=mesh_id,
        )

    rims = (
        (has_upper, me + GROUP, has_lower),
        (has_lower, me - GROUP, has_upper),
        (line_upper, me + 1, line_lower),
        (line_lower, me - 1, line_upper),
    )

    def send_rim(which):
        @pl.when(rims[which][0])
        def _():
            rim_copy(which, rims[which][1]).start()

    def await_rim(which):
        @pl.when(rims[which][2])
        def _():
            rim_copy(which, me).wait_recv()

    key_block = lax.div(lax.broadcasted_iota(jnp.int32, (1, WINDOW), 1), BLOCK)
    key_bit = jnp.left_shift(jnp.ones_like(key_block), key_block)

    def attend(queries, keys, values, head, block):
        lower = jnp.where((key_bit & table[head, block].astype(jnp.int32)) != 0, 0.0, MASKED)
        upper = jnp.where((key_bit & (table[head, block + 1].astype(jnp.int32) * 2)) != 0, 0.0, MASKED)
        bias = jnp.concatenate(
            [
                jnp.broadcast_to(lower, (BLOCK, WINDOW)),
                jnp.broadcast_to(upper, (BLOCK, WINDOW)),
            ],
            axis=0,
        )
        score = lax.dot_general(
            queries, keys, (((1,), (1,)), ((), ())), preferred_element_type=jnp.float32
        )
        score = score * table[head, logit_at] + bias
        peak = jnp.max(score, axis=-1, keepdims=True)
        weight = jnp.exp(score - peak)
        total = jnp.sum(weight, axis=-1, keepdims=True)
        mixed = jnp.dot(
            weight.astype(jnp.bfloat16), values, preferred_element_type=jnp.float32
        )
        return (mixed * (table[head, logit_at + 1] / total)).astype(jnp.bfloat16)

    def near_pair(i, pair):
        start = pl.multiple_of(pair * PAIR, PAIR)
        head = share * slot + i
        near_out[i, pl.ds(start, PAIR), :] = attend(
            near[i, pl.ds(start + RIM, PAIR), 0:WIDTH],
            near[i, pl.ds(start, WINDOW), WIDTH : 2 * WIDTH],
            near[i, pl.ds(start, WINDOW), 2 * WIDTH : 3 * WIDTH],
            head,
            group * (near_rows // BLOCK) + 2 * pair,
        )

    line_head = spatial + frame

    def line_pair(pair):
        start = pl.multiple_of(pair * PAIR, PAIR)
        line_out[pl.ds(start, PAIR), :] = attend(
            lines[pl.ds(start + RIM, PAIR), 0:WIDTH],
            lines[pl.ds(start, WINDOW), WIDTH : 2 * WIDTH],
            lines[pl.ds(start, WINDOW), 2 * WIDTH : 3 * WIDTH],
            line_head,
            chunk * (line_rows // BLOCK) + 2 * pair,
        )

    for step in range(1, GROUP):
        near_copy(near_peer(step), near_peer(step)).wait_recv()
    own_near.wait()
    table_copy.wait()
    send_rim(0)
    send_rim(1)

    def near_middle(n, carry):
        for i in range(share):
            near_pair(i, n + 1)
        return carry

    lax.fori_loop(0, near_pairs - 2, near_middle, 0)

    for step in range(1, FRAMES):
        far_copy(far_peer(step), far_peer(step)).wait_recv()
    own_far.wait()

    def turn(s, carry):
        piece = frames[:, pl.ds(pl.multiple_of(s * tile, tile), tile), :]
        lines[pl.ds(pl.multiple_of(RIM + s * strip, RIM), strip), :] = jnp.dot(
            swap[...], piece.reshape(strip, 3 * WIDTH), preferred_element_type=jnp.float32
        ).astype(jnp.bfloat16)
        return carry

    lax.fori_loop(0, strips, turn, 0)
    send_rim(2)
    send_rim(3)

    await_rim(0)
    await_rim(1)

    def near_edge(i, carry):
        near_pair(i, 0)
        near_pair(i, near_pairs - 1)
        return carry

    lax.fori_loop(0, share, near_edge, 0)

    def near_back(peer, source):
        return pltpu.make_async_remote_copy(
            src_ref=near_out.at[:, pl.ds(rows * peer, rows), :],
            dst_ref=returned.at[pl.ds(share * source, share)],
            send_sem=near_back_send.at[peer],
            recv_sem=near_back_recv.at[source],
            device_id=device(base + peer),
            device_id_type=mesh_id,
        )

    def far_back(peer, source):
        return pltpu.make_async_remote_copy(
            src_ref=frame_out.at[peer],
            dst_ref=returned.at[spatial + source],
            send_sem=far_back_send.at[peer],
            recv_sem=far_back_recv.at[source],
            device_id=device(peer * per_frame + chunk),
            device_id_type=mesh_id,
        )

    for step in range(1, GROUP):
        near_back(near_peer(step), slot).start()
    own_near_back = pltpu.make_async_copy(
        near_out.at[:, pl.ds(rows * slot, rows), :],
        returned.at[pl.ds(share * slot, share)],
        own_sem.at[2],
    )
    own_near_back.start()

    def line_middle(n, carry):
        line_pair(2 * n + 1)
        line_pair(2 * n + 2)
        return carry

    lax.fori_loop(0, (line_pairs - 2) // 2, line_middle, 0)
    await_rim(2)
    await_rim(3)
    line_pair(0)
    line_pair(line_pairs - 1)

    def turn_back(s, carry):
        piece = jnp.dot(
            swap[...],
            line_out[pl.ds(pl.multiple_of(s * strip, strip), strip), :],
            preferred_element_type=jnp.float32,
        ).astype(jnp.bfloat16)
        frame_out[:, pl.ds(pl.multiple_of(s * tile, tile), tile), :] = piece.reshape(
            FRAMES, tile, WIDTH
        )
        return carry

    lax.fori_loop(0, strips, turn_back, 0)
    for step in range(1, FRAMES):
        far_back(far_peer(step), frame).start()
    own_far_back = pltpu.make_async_copy(
        frame_out.at[frame], returned.at[spatial + frame], own_sem.at[3]
    )
    own_far_back.start()

    for step in range(1, GROUP):
        near_copy(near_peer(step), slot).wait_send()
        near_back(near_peer(step), slot).wait_send()
        near_back(near_peer(step), near_peer(step)).wait_recv()
    for which in range(4):

        @pl.when(rims[which][0])
        def _(which=which):
            rim_copy(which, rims[which][1]).wait_send()

    own_near_back.wait()
    for step in range(1, FRAMES):
        far_copy(far_peer(step), frame).wait_send()
        far_back(far_peer(step), frame).wait_send()
        far_back(far_peer(step), far_peer(step)).wait_recv()
    own_far_back.wait()


def shards(
    devices,
    queries,
    key_vectors,
    value_vectors,
    labels,
    block_lists,
    counts,
    query_scale,
    key_scale,
    value_scale,
):
    rows, width = queries.shape
    heads = labels.shape[0]
    blocks = counts.shape[1]
    spatial = heads - TEMPORAL
    share = spatial // GROUP
    ulysses = lax.axis_size("ulysses")

    near_rows = GROUP * rows
    line_rows = FRAMES * rows
    bf16 = jnp.bfloat16
    vmem = pl.BlockSpec(memory_space=pltpu.VMEM)
    anywhere = pl.BlockSpec(memory_space=pl.ANY)
    hbm = pl.BlockSpec(memory_space=pltpu.HBM)
    lists = jnp.transpose(block_lists, (2, 0, 1))
    table_width = -(-blocks // WIDTH) * WIDTH + WIDTH
    packed, table = pl.pallas_call(
        pack,
        out_shape=(
            jax.ShapeDtypeStruct((heads, rows, 3 * WIDTH), bf16),
            jax.ShapeDtypeStruct((heads, table_width), jnp.float32),
        ),
        in_specs=[hbm] * 9,
        out_specs=(vmem, vmem),
        scratch_shapes=[
            pltpu.SMEM((heads,), jnp.int32),
            pltpu.SMEM((heads,), jnp.float32),
            pltpu.SMEM((heads,), jnp.float32),
            pltpu.SMEM((heads,), jnp.float32),
            pltpu.VMEM(lists.shape, jnp.int32),
            pltpu.VMEM((heads, blocks), jnp.int32),
            pltpu.VMEM((heads, table_width), jnp.float32),
            pltpu.SemaphoreType.DMA((6,)),
            pltpu.SemaphoreType.DMA,
        ],
        compiler_params=pltpu.CompilerParams(vmem_limit_bytes=60 * 1024 * 1024),
    )(
        labels,
        query_scale,
        key_scale,
        value_scale,
        lists,
        counts,
        queries,
        key_vectors,
        value_vectors,
    )
    returned = pl.pallas_call(
        functools.partial(kernel, devices, ulysses),
        out_shape=jax.ShapeDtypeStruct((heads, rows, WIDTH), bf16),
        in_specs=[anywhere] * 2,
        out_specs=anywhere,
        scratch_shapes=[
            pltpu.SMEM((heads, table_width), jnp.float32),
            pltpu.VMEM((share, near_rows + 2 * RIM, 3 * WIDTH), bf16),
            pltpu.VMEM((FRAMES, rows, 3 * WIDTH), bf16),
            pltpu.VMEM((line_rows + 2 * RIM, 3 * WIDTH), bf16),
            pltpu.VMEM((share, near_rows, WIDTH), bf16),
            pltpu.VMEM((line_rows, WIDTH), bf16),
            pltpu.VMEM((FRAMES, rows, WIDTH), bf16),
            pltpu.VMEM((16 * FRAMES, 16 * FRAMES), bf16),
            pltpu.SemaphoreType.DMA((GROUP,)),
            pltpu.SemaphoreType.DMA((GROUP,)),
            pltpu.SemaphoreType.DMA((FRAMES,)),
            pltpu.SemaphoreType.DMA((FRAMES,)),
            pltpu.SemaphoreType.DMA((4,)),
            pltpu.SemaphoreType.DMA((4,)),
            pltpu.SemaphoreType.DMA((4,)),
            pltpu.SemaphoreType.DMA((GROUP,)),
            pltpu.SemaphoreType.DMA((GROUP,)),
            pltpu.SemaphoreType.DMA((FRAMES,)),
            pltpu.SemaphoreType.DMA((FRAMES,)),
            pltpu.SemaphoreType.DMA,
        ],
        compiler_params=pltpu.CompilerParams(
            collective_id=0, has_side_effects=True, vmem_limit_bytes=60 * 1024 * 1024
        ),
        cost_estimate=pl.CostEstimate(
            flops=10**9, bytes_accessed=4 * rows * width * 2, transcendentals=10**6
        ),
    )(table, packed)
    return pl.pallas_call(
        unpack,
        out_shape=jax.ShapeDtypeStruct((rows, width), bf16),
        in_specs=[hbm, anywhere],
        out_specs=hbm,
        compiler_params=pltpu.CompilerParams(vmem_limit_bytes=8 * 1024 * 1024),
        scratch_shapes=[
            pltpu.SMEM((heads,), jnp.int32),
            pltpu.SemaphoreType.DMA,
            pltpu.SemaphoreType.DMA,
        ],
    )(labels, returned)


def solution(mesh):
    tokens = P(("context", "ulysses"), None)
    devices = mesh.shape["ulysses"] * mesh.shape["context"]
    return jax.shard_map(
        functools.partial(shards, devices),
        mesh=mesh,
        in_specs=(tokens, tokens, tokens, P(), P(), P(), P(), P(), P()),
        out_specs=tokens,
        check_vma=False,
    )
```
